128 devices in a mesh: fsdp: 32 (over z, y, x_lo), tp: 4 (over x_hi, core).
Axes of the slice: x: 4 (x_hi: 2, x_lo: 2; x = x_hi * 2 + x_lo), y: 4, z: 4, core: 2. Of those that a mesh axis runs over, the one named last changes fastest.
Arguments:
- layer_input: float32 [32768, 1024], P(('fsdp', 'tp')), may hold values from -6 to 6
- cotangent: float32 [32768, 1024], P(('fsdp', 'tp')), may hold values from -24 to 24
- parents: int32 [32, 7], P('fsdp'), may hold values from 0 to 4, as said below
- offsets: int32 [32, 7], P('fsdp'), may hold values from 0 to 960, as said below
- w_query: bfloat16 [1024, 2048], P('fsdp', 'tp'), may hold values from -0.1875 to 0.1875
- w_key: bfloat16 [1024, 1024], P('fsdp', 'tp'), may hold values from -0.1875 to 0.1875
- w_value: bfloat16 [1024, 1024], P('fsdp', 'tp'), may hold values from -0.1875 to 0.1875
- w_output: bfloat16 [2048, 1024], P('tp', 'fsdp'), may hold values from -1 to 1
- w_gate: bfloat16 [1024, 3072], P('fsdp', 'tp'), may hold values from -0.1875 to 0.1875
- w_up: bfloat16 [1024, 3072], P('fsdp', 'tp'), may hold values from -0.1875 to 0.1875
- w_down: bfloat16 [3072, 1024], P('tp', 'fsdp'), may hold values from -0.109375 to 0.109375
- norm_attn: float32 [1024], P(('fsdp', 'tp')), may hold values from 0.1 to 1.9
- norm_mlp: float32 [1024], P(('fsdp', 'tp')), may hold values from 0.1 to 1.9
- query_gain: float32 [128], replicated, may hold values from 0.7 to 2
- key_gain: float32 [128], replicated, may hold values from 0.7 to 2
Outputs:
- layer_output: float32 [32768, 1024], P(('fsdp', 'tp'))
- input_grad: float32 [32768, 1024], P(('fsdp', 'tp'))
- w_query_grad: float32 [1024, 2048], P('fsdp', 'tp')
- w_key_grad: float32 [1024, 1024], P('fsdp', 'tp')
- w_value_grad: float32 [1024, 1024], P('fsdp', 'tp')
- w_output_grad: float32 [2048, 1024], P('tp', 'fsdp')
- w_gate_grad: float32 [1024, 3072], P('fsdp', 'tp')
- w_up_grad: float32 [1024, 3072], P('fsdp', 'tp')
- w_down_grad: float32 [3072, 1024], P('tp', 'fsdp')
- norm_attn_grad: float32 [1024], P(('fsdp', 'tp'))
- norm_mlp_grad: float32 [1024], P(('fsdp', 'tp'))
- query_gain_grad: float32 [128], replicated
- key_gain_grad: float32 [128], replicated
The draws below stay inside these ranges and needn't reach their ends.
Inputs may be any that keep to these rules, and one draw needn't show every extreme that they name: `parents`: in every tree segment 0 is the trunk and its own parent; every other segment's parent comes before it; two segments have parent 0, and each of them is the parent of two segments that are no segment's parent. offsets[b][0] = 0 and offsets rise; segment s of a tree covers positions offsets[s] to offsets[s+1] - 1 (the last one up to 1023); every segment but the trunk holds 64 to 128 positions.
All inputs are finite; a program needn't handle non-finite values.
Results may differ from the reference program's by a relative error of at most 0.035.
Values may be sent and summed in bfloat16 or wider, within the bound.
No kernel may reach another device: no remote copies, remote signals or barrier semaphores. Data moves between devices by JAX's collectives and lax.ppermute only.
A program may use at most 128 MiB of HBM per device.

```python
import math
import jax
import jax.numpy as jnp
from jax import lax

D = 1024
FF = 3072
H = 16
KVH = 8
HD = 128
TREE = 1024
TOKENS = 32768
N_TP = 4


def tree_layout(key):
    tree_count = TOKENS // TREE
    chosen = jax.random.randint(jax.random.fold_in(key, 77), (), 0, tree_count)
    forced_flags = jnp.arange(tree_count, dtype=jnp.int32) == chosen

    def one_tree(tree_key, forced):
        order_key, length_key = jax.random.split(tree_key)
        unit_rows = TREE // 16
        branch_rank = jax.random.randint(order_key, (2,), 0, 64)
        branch_rank = jnp.where(forced, jnp.array([0, 200], jnp.int32), branch_rank)
        leaf_rank = branch_rank[jnp.array([0, 0, 1, 1])] + jax.random.randint(jax.random.fold_in(order_key, 1), (4,), 1, 64)
        node_score = jnp.concatenate([branch_rank, leaf_rank]) * 8 + jnp.arange(6, dtype=jnp.int32)
        layout_order = jnp.argsort(node_score, stable=True).astype(jnp.int32)
        node_place = jnp.argsort(layout_order, stable=True).astype(jnp.int32)
        node_parent = jnp.array([-1, -1, 0, 0, 1, 1], jnp.int32)
        parent_node = node_parent[layout_order]
        rest_parents = jnp.where(parent_node < 0, 0, 1 + node_place[jnp.maximum(parent_node, 0)])
        parents = jnp.concatenate([jnp.zeros((1,), jnp.int32), rest_parents.astype(jnp.int32)])
        rest_rows = unit_rows + jax.random.randint(length_key, (6,), 0, unit_rows + 1)
        trunk_rows = 16 * unit_rows - jnp.sum(rest_rows)
        segment_rows = jnp.concatenate([trunk_rows[None], rest_rows]).astype(jnp.int32)
        offsets = jnp.concatenate([jnp.zeros((1,), jnp.int32), jnp.cumsum(segment_rows)[:-1].astype(jnp.int32)])
        return (parents, offsets)
    return jax.vmap(one_tree)(jax.random.split(key, tree_count), forced_flags)


def draw_parents(key, part):
    return tree_layout(key)[0]


def draw_offsets(key, part):
    return tree_layout(key)[1]


def strengthened(values, stream_key, source, target, blocks, factor):
    owner, partner = [(jnp.arange(values.shape[dim]) // (values.shape[dim] // blocks)).reshape([-1 if axis == dim else 1 for axis in range(values.ndim)]) for dim in (source, target)]
    chosen = jax.random.permutation(stream_key, blocks)[partner]
    strong = (owner == chosen) | (owner == (partner + blocks // 2) % blocks)
    return jnp.where(strong, factor * values, values)


def levels(key, shape, cuts, smallest, top_value):
    gain, own = 1.0, jax.random.fold_in(key, 6)
    for dim, shards_of in cuts:
        heights = jnp.exp(jax.random.uniform(jax.random.fold_in(own, dim), (shards_of,), jnp.float32, smallest / len(cuts), top_value / len(cuts)))
        gain = gain * jnp.repeat(heights, shape[dim] // shards_of).reshape([-1 if axis == dim else 1 for axis in range(len(shape))])
    return gain


def normal_values(key, extent, spread, reach, pieces=(), held_as=jnp.bfloat16):
    factor_of = levels(key, extent, pieces, -0.22, 0.18) if pieces else 1.0
    entries = jax.random.normal(key, extent, jnp.float32) * spread * factor_of
    return jnp.minimum(jnp.maximum(entries, -reach), reach).astype(held_as)


def gaussian_with(stream_key, shape, scale, reach, cuts, heavy, kind=jnp.bfloat16):
    entries = scale * jax.random.normal(stream_key, shape, jnp.float32)
    if cuts:
        entries = entries * levels(stream_key, shape, cuts, -0.22, 0.18)
    return jnp.clip(strengthened(entries, jax.random.fold_in(stream_key, 3), *heavy), -reach, reach).astype(kind)


def setup_inputs(seed: int = 0) -> dict:
    seeds = jax.random.split(jax.random.key(seed), 16)
    return {
        "layer_input": normal_values(seeds[0], (TOKENS, D), 1.0, 6.0, ((0, 128),), jnp.float32),
        "cotangent": gaussian_with(seeds[1], (TOKENS, D), 1.0, 24.0, ((0, 128),), (0, 1, 128, 5.5), jnp.float32),
        "parents": draw_parents(jax.random.fold_in(seeds[15], 71), 0),
        "offsets": draw_offsets(jax.random.fold_in(seeds[15], 71), 0),
        "w_query": normal_values(seeds[4], (D, H * HD), D ** -0.5, 0.1875, ((0, 32), (1, 4))),
        "w_key": normal_values(seeds[5], (D, KVH * HD), D ** -0.5, 0.1875, ((0, 32), (1, 4))),
        "w_value": normal_values(seeds[6], (D, KVH * HD), D ** -0.5, 0.1875, ((0, 32), (1, 4))),
        "w_output": normal_values(seeds[7], (H * HD, D), (H * HD // 64) ** -0.5, 1.0, ((0, 4), (1, 32))),
        "w_gate": normal_values(seeds[8], (D, FF), D ** -0.5, 0.1875, ((0, 32), (1, 4))),
        "w_up": normal_values(seeds[9], (D, FF), D ** -0.5, 0.1875, ((0, 32), (1, 4))),
        "w_down": normal_values(seeds[10], (FF, D), FF ** -0.5, 0.109375, ((0, 4), (1, 32))),
        "norm_attn": jnp.clip(1.0 + 0.18 * jax.random.normal(seeds[11], (D,), jnp.float32), 0.1, 1.9),
        "norm_mlp": jnp.clip(1.0 + 0.18 * jax.random.normal(seeds[12], (D,), jnp.float32), 0.1, 1.9),
        "query_gain": jnp.clip(jnp.exp(jax.random.uniform(seeds[13], (HD,), jnp.float32, math.log(0.7), math.log(2.0))), 0.7, 2.0),
        "key_gain": jnp.clip(jnp.exp(jax.random.uniform(seeds[14], (HD,), jnp.float32, math.log(0.7), math.log(2.0))), 0.7, 2.0),
    }


EPSILON = 1e-06
THETA = 1000000.0
MASKED = -1e+30

@jax.custom_vjp
def low(v):
    return lax.optimization_barrier(v.astype(jnp.bfloat16)).astype(jnp.float32)

@jax.custom_vjp
def low_back(v):
    return v

def low_keep(v):
    return (low(v), None)

def low_pass(kept, grad):
    return (grad,)

def back_keep(v):
    return (v, None)

def back_low(kept, grad):
    return (low(grad),)
low.defvjp(low_keep, low_pass)
low_back.defvjp(back_keep, back_low)

def matmul(left, right):
    return jnp.dot(left, right, precision=lax.Precision.HIGHEST)

def normalize(rows):
    return rows * lax.rsqrt(lax.optimization_barrier(jnp.mean(rows * rows, axis=-1, keepdims=True)) + EPSILON)

def tree_tables(parents, offsets, tree_rows):
    positions = jnp.arange(tree_rows, dtype=jnp.int32)
    labels = jnp.arange(parents.shape[0], dtype=jnp.int32)
    segment = lax.optimization_barrier(jnp.sum((positions[:, None] >= offsets[None, 1:]).astype(jnp.int32), axis=1))
    member = segment[:, None] == labels[None, :]
    parent_pick = parents[:, None] == labels[None, :]
    grandparent = lax.optimization_barrier(jnp.sum(jnp.where(parent_pick, parents[None, :], 0), axis=1))
    ancestry = (labels[None, :] == labels[:, None]) | (labels[None, :] == parents[:, None]) | (labels[None, :] == grandparent[:, None])
    segment_ends = jnp.concatenate([offsets[1:], jnp.full((1,), tree_rows, jnp.int32)])
    lengths = segment_ends - offsets
    parent_len = lax.optimization_barrier(jnp.sum(jnp.where(parent_pick, lengths[None, :], 0), axis=1))
    grand_pick = grandparent[:, None] == labels[None, :]
    grand_len = lax.optimization_barrier(jnp.sum(jnp.where(grand_pick, lengths[None, :], 0), axis=1))
    path_start = jnp.where(labels > 0, parent_len, 0) + jnp.where(parents > 0, grand_len, 0)
    path_position = positions + lax.optimization_barrier(jnp.sum(jnp.where(member, (path_start - offsets)[None, :], 0), axis=1))
    row_ancestry = jnp.any(member[:, :, None] & ancestry[None, :, :], axis=1)
    reachable = jnp.any(row_ancestry[:, None, :] & member[None, :, :], axis=-1)
    allowed = reachable & (positions[None, :] <= positions[:, None])
    return (allowed, path_position)

def rotary(path_position):
    frequency = jnp.exp(jnp.arange(0, HD, 2).astype(jnp.float32) * (-math.log(THETA) / HD))
    angles = path_position.astype(jnp.float32)[:, None] * frequency[None, :]
    cosine_table = jnp.concatenate([jnp.cos(angles), jnp.cos(angles)], axis=1)[:, None, :]
    sine_table = jnp.concatenate([jnp.sin(angles), jnp.sin(angles)], axis=1)[:, None, :]
    return (cosine_table, sine_table)

def rope(rows, cosine_table, sine_table):
    half_width = rows.shape[-1] // 2
    turned = jnp.concatenate([-rows[..., half_width:], rows[..., :half_width]], axis=-1)
    return rows * cosine_table + turned * sine_table

def tree_layer(rows, tree_parents, tree_offsets, w_query, w_key, w_value, w_output, w_gate, w_up, w_down, norm_attn, norm_mlp, query_gain, key_gain):
    tree_rows = rows.shape[0]
    groups = N_TP
    query_cols = H * HD // groups
    key_cols = KVH * HD // groups
    ff_cols = FF // groups
    allowed, path_position = tree_tables(tree_parents, tree_offsets, tree_rows)
    cosine_table, sine_table = rotary(path_position)
    first_rows = low(normalize(rows) * norm_attn)
    query_parts = []
    key_parts = []
    value_parts = []
    for group in range(groups):
        first_copy = low_back(first_rows)
        query_parts.append(low_back(matmul(first_copy, w_query[:, group * query_cols:(group + 1) * query_cols])))
        key_parts.append(low_back(matmul(first_copy, w_key[:, group * key_cols:(group + 1) * key_cols])))
        value_parts.append(low_back(matmul(first_copy, w_value[:, group * key_cols:(group + 1) * key_cols])))
    query_raw = jnp.concatenate(query_parts, axis=1).reshape(tree_rows, H, HD)
    key_raw = jnp.concatenate(key_parts, axis=1).reshape(tree_rows, KVH, HD)
    values = low(jnp.concatenate(value_parts, axis=1)).reshape(tree_rows, KVH, HD)
    queries = low(rope(normalize(query_raw) * query_gain, cosine_table, sine_table))
    key_rows = low(rope(normalize(key_raw) * key_gain, cosine_table, sine_table))
    grouped = queries.reshape(tree_rows, KVH, H // KVH, HD)
    scores = jnp.einsum('rgqd,kgd->gqrk', grouped, key_rows, precision=lax.Precision.HIGHEST) * (1.0 / math.sqrt(HD))
    scores = low_back(scores)
    scores = jnp.where(allowed[None, None], scores, MASKED)
    row_max = lax.optimization_barrier(jnp.max(scores, axis=-1, keepdims=True))
    exponent = jnp.exp(scores - row_max)
    soft_weights = exponent / lax.optimization_barrier(jnp.sum(exponent, axis=-1, keepdims=True))
    mixed_rows = jnp.einsum('gqrk,kgd->rgqd', low(soft_weights), values, precision=lax.Precision.HIGHEST)
    attended = low(low_back(mixed_rows.reshape(tree_rows, H * HD)))
    attn_total = jnp.zeros(rows.shape, jnp.float32)
    for group in range(groups):
        attn_total = attn_total + low(matmul(attended[:, group * query_cols:(group + 1) * query_cols], w_output[group * query_cols:(group + 1) * query_cols, :]))
    mid_rows = rows + low_back(attn_total)
    second_rows = low(normalize(mid_rows) * norm_mlp)
    gate_parts = []
    up_parts = []
    for group in range(groups):
        second_copy = low_back(second_rows)
        gate_parts.append(low_back(matmul(second_copy, w_gate[:, group * ff_cols:(group + 1) * ff_cols])))
        up_parts.append(low_back(matmul(second_copy, w_up[:, group * ff_cols:(group + 1) * ff_cols])))
    gate_rows = jnp.concatenate(gate_parts, axis=1)
    up_rows = jnp.concatenate(up_parts, axis=1)
    activated = low(gate_rows * jax.nn.sigmoid(gate_rows) * up_rows)
    mlp_total = jnp.zeros(rows.shape, jnp.float32)
    for group in range(groups):
        mlp_total = mlp_total + low(matmul(activated[:, group * ff_cols:(group + 1) * ff_cols], w_down[group * ff_cols:(group + 1) * ff_cols, :]))
    return mid_rows + low_back(mlp_total)

def reference(layer_input, cotangent, parents, offsets, w_query, w_key, w_value, w_output, w_gate, w_up, w_down, norm_attn, norm_mlp, query_gain, key_gain):

    def whole(inputs, wq_float, wk_float, wv_float, wo_float, wg_float, wu_float, wd_float, gain_attn, gain_mlp, gain_query, gain_key):
        layer = jax.checkpoint(tree_layer)

        def one_tree(item):
            tree_input, tree_parents, tree_offsets = item
            return layer(tree_input, tree_parents, tree_offsets, wq_float, wk_float, wv_float, wo_float, wg_float, wu_float, wd_float, gain_attn, gain_mlp, gain_query, gain_key)
        trees = inputs.reshape(parents.shape[0], -1, inputs.shape[1])
        return lax.map(one_tree, (trees, parents, offsets)).reshape(inputs.shape)
    result, pullback = jax.vjp(whole, layer_input, w_query.astype(jnp.float32), w_key.astype(jnp.float32), w_value.astype(jnp.float32), w_output.astype(jnp.float32), w_gate.astype(jnp.float32), w_up.astype(jnp.float32), w_down.astype(jnp.float32), norm_attn, norm_mlp, query_gain, key_gain)
    grads = pullback(cotangent)
    return (result, grads[0], grads[1], grads[2], grads[3], grads[4], grads[5], grads[6], grads[7], grads[8], grads[9], grads[10], grads[11])
```

```python
import functools
import math

import jax
import jax.numpy as jnp
from jax import lax
from jax.experimental import pallas as pl
from jax.experimental.pallas import tpu as pltpu
from jax.sharding import PartitionSpec as P

H = 16
KVH = 8
HD = 128
GROUP = 4
ROWS = 256
HEADS = H // GROUP
Z, Y, X = 4, 4, 2
PART = 64
KV = KVH // GROUP
Q_WIDTH = HEADS * HD
K_WIDTH = KV * HD

EPSILON = 1e-06
THETA = 1000000.0
BARRED = -512.0
LOG2E = 1.0 / math.log(2.0)
SCALE = 1.0 / math.sqrt(HD)
MIB = 1024 * 1024
BF16 = jnp.bfloat16
F32 = jnp.float32


def tree_tables(parents, offsets, tree_rows):
    positions = jnp.arange(tree_rows, dtype=jnp.int32)
    labels = jnp.arange(parents.shape[0], dtype=jnp.int32)
    segment = jnp.sum((positions[:, None] >= offsets[None, 1:]).astype(jnp.int32), axis=1)
    member = segment[:, None] == labels[None, :]
    parent_pick = parents[:, None] == labels[None, :]
    grandparent = jnp.sum(jnp.where(parent_pick, parents[None, :], 0), axis=1)
    ancestry = (
        (labels[None, :] == labels[:, None])
        | (labels[None, :] == parents[:, None])
        | (labels[None, :] == grandparent[:, None])
    )
    segment_ends = jnp.concatenate([offsets[1:], jnp.full((1,), tree_rows, jnp.int32)])
    lengths = segment_ends - offsets
    parent_len = jnp.sum(jnp.where(parent_pick, lengths[None, :], 0), axis=1)
    grand_pick = grandparent[:, None] == labels[None, :]
    grand_len = jnp.sum(jnp.where(grand_pick, lengths[None, :], 0), axis=1)
    path_start = jnp.where(labels > 0, parent_len, 0) + jnp.where(parents > 0, grand_len, 0)
    path_position = positions + jnp.sum(
        jnp.where(member, (path_start - offsets)[None, :], 0), axis=1
    )
    member_float = member.astype(F32)
    row_ancestry = jnp.dot(member_float, ancestry.astype(F32), preferred_element_type=F32)
    return (row_ancestry, member_float, path_position)


def score_terms(row_ancestry, member):
    spare = HD - member.shape[1]
    query_extra = jnp.pad((1.0 - row_ancestry) * BARRED, ((0, 0), (0, spare)))
    column = jnp.arange(HD, dtype=jnp.int32)[None, :]
    key_extra = jnp.pad(member, ((0, 0), (0, spare)))
    key_extra = jnp.where((column >= 8) & (column <= 10), 1.0, key_extra)
    return query_extra.astype(BF16), key_extra.astype(BF16)


def rotary(path_position):
    frequency = jnp.exp(jnp.arange(0, HD, 2).astype(F32) * (-math.log(THETA) / HD))
    angles = path_position.astype(F32)[:, None] * frequency[None, :]
    cosine, sine = jnp.cos(angles), jnp.sin(angles)
    return jnp.concatenate([cosine, cosine], axis=1), jnp.concatenate([-sine, sine], axis=1)


def norm_back(gradient, normed, inverse):
    return inverse * (gradient - normed * jnp.mean(gradient * normed, axis=-1, keepdims=True))


def flip(bits):
    return [(t, t ^ bits) for t in range(GROUP)]


def swap_x():
    return [(f, f ^ 1) for f in range(Z * Y * X)]


def planes():
    return [[(z * Y + y) * X + x for z in range(Z) for y in range(Y)] for x in range(X)]


def swapped(value):
    return lax.ppermute(value, "fsdp", swap_x())


def in_order(own, other):
    second = lax.axis_index("fsdp") % X == 1
    return jnp.concatenate(
        [jnp.where(second, other, own), jnp.where(second, own, other)], axis=0
    )


def gather_plane(pair):
    return lax.all_gather(pair, "fsdp", axis=0, tiled=True, axis_index_groups=planes())


def scatter_plane(partial):
    return lax.psum_scatter(
        partial, "fsdp", scatter_dimension=0, tiled=True, axis_index_groups=planes()
    )


def line(dim, step):
    pairs = []
    for z in range(Z):
        for y in range(Y):
            for x in range(X):
                far_z = (z + step) % Z if dim == "z" else z
                far_y = (y + step) % Y if dim == "y" else y
                pairs.append(((z * Y + y) * X + x, (far_z * Y + far_y) * X + x))
    return pairs


def lines(dim):
    if dim == "z":
        return [[(z * Y + y) * X + x for z in range(Z)] for y in range(Y) for x in range(X)]
    return [[(z * Y + y) * X + x for y in range(Y)] for z in range(Z) for x in range(X)]


def send_line(blocks, dim):
    return [blocks[0]] + [
        lax.ppermute(blocks[k], "fsdp", line(dim, k)) for k in range(1, 4)
    ]


def add_line(blocks):
    return sum(block.astype(F32) for block in blocks).astype(BF16)


def scatter_line(total, dim):
    parts = total.reshape(4, -1, total.shape[1])
    parts = lax.all_to_all(parts, "fsdp", 0, 0, tiled=True, axis_index_groups=lines(dim))
    return jnp.sum(parts.astype(F32), axis=0)


def exchange_plane(blocks):
    return lax.all_to_all(blocks, "fsdp", 0, 0, tiled=True, axis_index_groups=planes())


def scatter_pair(total):
    here = lax.axis_index("fsdp") % X
    halves = total.reshape(X, -1, total.shape[1])
    keep = lax.dynamic_index_in_dim(halves, here, 0, keepdims=False)
    send = lax.dynamic_index_in_dim(halves, 1 - here, 0, keepdims=False)
    return keep.astype(F32) + swapped(send.astype(BF16)).astype(F32)


def gather_rows(rows):
    across = lax.ppermute(rows, "tp", flip(2))
    beside = lax.ppermute(rows, "tp", flip(1))
    far = lax.ppermute(across, "tp", flip(1))
    return rows, beside, across, far


def add_cores(keep, received):
    other = (keep[1].astype(F32) + received[1].astype(F32)).astype(BF16)
    other, keep, received = lax.optimization_barrier((other, keep, received))
    return keep[0].astype(F32) + received[0].astype(F32), other


def scatter_chips(own, other):
    return own + lax.ppermute(other, "tp", flip(2)).astype(F32)


def scatter_rows(keep, send):
    return scatter_chips(*add_cores(keep, lax.ppermute(send, "tp", flip(1))))


def gather_small(values):
    me = lax.axis_index("tp")
    total = jnp.zeros((GROUP,) + values.shape, values.dtype)
    for bits in range(GROUP):
        piece = values if bits == 0 else lax.ppermute(values, "tp", flip(bits))
        total = lax.dynamic_update_index_in_dim(total, piece, me ^ bits, 0)
    return jnp.swapaxes(total, 0, 1).reshape(values.shape[0], -1)


def gather_gains(values):
    fsdp = lax.axis_size("fsdp")
    copies = jnp.broadcast_to(values.reshape(1, 1, -1), (fsdp, 1, values.size))
    full = lax.all_to_all(copies, "fsdp", 0, 0, tiled=True)
    full = full.reshape(fsdp, *values.shape)
    return jnp.swapaxes(full, 0, 1).reshape(values.shape[0], -1)


def sum_group(values):
    return values + sum(lax.ppermute(values, "tp", flip(bits)) for bits in range(1, GROUP))


def nn(left, right):
    return lax.dot_general(left, right, (((1,), (0,)), ((), ())), preferred_element_type=F32)


def nt(left, right):
    return lax.dot_general(left, right, (((1,), (1,)), ((), ())), preferred_element_type=F32)


def tn(left, right):
    return lax.dot_general(left, right, (((0,), (0,)), ((), ())), preferred_element_type=F32)


def block(index):
    return pl.ds(index * ROWS, ROWS)


def dynamic_block(index):
    return pl.ds(pl.multiple_of(index * ROWS, ROWS), ROWS)


def three_terms(value):
    high = value.astype(BF16)
    rest = value - high.astype(F32)
    middle = rest.astype(BF16)
    return high, middle, (rest - middle.astype(F32)).astype(BF16)


def lanes_of(shape):
    return lax.broadcasted_iota(jnp.int32, shape, 1)


class Copies:
    def __init__(self, semaphores):
        self.semaphores, self.used, self.open = semaphores, 0, []

    def start(self, source, target):
        copy = pltpu.make_async_copy(source, target, self.semaphores.at[self.used])
        self.used += 1
        copy.start()
        self.open.append(copy)
        return copy

    def start_choice(self, source, evens, odds, index):
        semaphore = self.semaphores.at[self.used]
        self.used += 1
        for bit, target in ((0, evens), (1, odds)):

            @pl.when(index % 2 == bit)
            def _():
                pltpu.make_async_copy(source, target.at[index // 2], semaphore).start()

        self.open.append(pltpu.make_async_copy(source, evens.at[0], semaphore))

    def finish(self, copies=None):
        for copy in list(self.open) if copies is None else copies:
            copy.wait()
            self.open = [other for other in self.open if other is not copy]


def turn(rows):
    return pltpu.roll(rows, HD // 2, 1)


def attention_kernel(
    place_ref,
    piece0,
    piece1,
    piece2,
    piece3,
    in_hbm,
    cosine_hbm,
    sine_hbm,
    query_extra_hbm,
    key_extra_hbm,
    gain_ref,
    row_gain_ref,
    queries_hbm,
    keys_hbm,
    values_hbm,
    attended_hbm,
    query_hat_hbm,
    key_hat_hbm,
    inverse_hbm,
    rows_hbm,
    keep_hbm,
    send_hbm,
    rows,
    w_in,
    w_out,
    cosine,
    sine,
    query_extra,
    key_extra,
    queries,
    keys,
    values,
    attended,
    query_hat,
    key_hat,
    inverse,
    partial,
    semaphores,
):
    me = place_ref[0]
    copies = Copies(semaphores)
    pieces = (piece0, piece1, piece2, piece3)
    in_width = w_in.shape[1]
    first = [copies.start(in_hbm.at[:, :in_width], w_in)]
    for bits, piece in enumerate(pieces):
        first.append(copies.start(piece, rows.at[dynamic_block(me ^ bits)]))
    for source, target in (
        (cosine_hbm, cosine),
        (sine_hbm, sine),
        (query_extra_hbm, query_extra),
        (key_extra_hbm, key_extra),
    ):
        first.append(copies.start(source, target))
    out_copy = copies.start(in_hbm.at[:, in_width : in_width + Q_WIDTH], w_out)
    copies.finish(first)
    for bits in range(GROUP):
        copies.start(rows.at[dynamic_block(me ^ bits)], rows_hbm.at[block(bits)])
    query_gain = gain_ref[0:1, :] * (SCALE * LOG2E)
    key_gain = gain_ref[1:2, :]
    lane = lanes_of((ROWS, HD))
    for g in range(KV):
        values[g, :, HD:] = jnp.ones((GROUP * ROWS, HD), BF16)
        keys[g, :, HD:] = key_extra[...]
    causal = lax.broadcasted_iota(jnp.int32, (ROWS, ROWS), 0) >= lax.broadcasted_iota(
        jnp.int32, (ROWS, ROWS), 1
    )
    causal = jnp.concatenate([causal] * (HEADS // KV), axis=0)

    for i in range(GROUP):
        here = block(i)
        there = me ^ i
        gained = (rows[here, :].astype(F32) * row_gain_ref[0:1, :]).astype(BF16)
        projected = nn(gained, w_in[...])
        cos, sin = cosine[here, :], sine[here, :]
        inverses = jnp.zeros((ROWS, HD), F32)
        for j in range(HEADS + KV):
            raw = projected[:, j * HD : (j + 1) * HD]
            scale = lax.rsqrt(jnp.mean(raw * raw, axis=1, keepdims=True) + EPSILON)
            inverses = jnp.where(lane == j, scale, inverses)
            hat = raw * scale
            gained = hat * (query_gain if j < HEADS else key_gain)
            roped = (gained * cos + turn(gained) * sin).astype(BF16)
            if j < HEADS:
                query_hat[here, j * HD : (j + 1) * HD] = hat.astype(BF16)
                queries[j, here, :HD] = roped
                queries[j, here, HD:] = query_extra[here, :]
            else:
                g = j - HEADS
                key_hat[here, g * HD : (g + 1) * HD] = hat.astype(BF16)
                keys[g, here, :HD] = roped
        inverse[here, :] = inverses
        for g in range(KV):
            start = Q_WIDTH + K_WIDTH + g * HD
            values[g, here, :HD] = projected[:, start : start + HD].astype(BF16)
        parts = []
        for g in range(KV):
            both = queries[2 * g : 2 * g + 2, here, :].reshape(2 * ROWS, 2 * HD)
            mixed = None
            for kb in range(i + 1):
                weights = jnp.exp2(nt(both, keys[g, block(kb), :]))
                if kb == i:
                    weights = jnp.where(causal, weights, 0.0)
                part = nn(weights.astype(BF16), values[g, block(kb), :])
                mixed = part if mixed is None else mixed + part
            total = mixed[:, HD:]
            out = (mixed[:, :HD] / total).astype(BF16)
            logs = three_terms(-jnp.log2(total))
            for hh in range(2):
                h = 2 * g + hh
                parts.append(out[hh * ROWS : (hh + 1) * ROWS])
                extra = queries[h, here, HD:]
                for k, term in enumerate(logs):
                    extra = jnp.where(lane == 8 + k, term[hh * ROWS : (hh + 1) * ROWS], extra)
                queries[h, here, HD:] = extra
        mixed_rows = jnp.concatenate(parts, axis=1)
        attended[here, :] = mixed_rows
        if i == 0:
            copies.finish([out_copy])
        partial[i] = nt(mixed_rows, w_out[...]).astype(BF16)
        copies.start_choice(partial.at[i], keep_hbm, send_hbm, there)
        copies.start(attended.at[here], attended_hbm.at[dynamic_block(there)])
        copies.start(query_hat.at[here], query_hat_hbm.at[here])
        copies.start(key_hat.at[here], key_hat_hbm.at[here])
        copies.start(inverse.at[here], inverse_hbm.at[here])
        for h in range(HEADS):
            copies.start(queries.at[h, here], queries_hbm.at[h, here])
        for g in range(KV):
            copies.start(keys.at[g, here], keys_hbm.at[g, here])
            copies.start(values.at[g, here], values_hbm.at[g, here])
    copies.finish()


def mlp_kernel(
    row0,
    row1,
    row2,
    row3,
    low0,
    low1,
    low2,
    low3,
    rest_hbm,
    row_gain_ref,
    rows_hbm,
    low_hbm,
    active_hbm,
    grads_hbm,
    keep_hbm,
    send_hbm,
    rows,
    low,
    mix,
    down,
    active,
    grads,
    partial,
    semaphores,
):
    copies = Copies(semaphores)
    width = down.shape[1]
    row_pieces, low_pieces = (row0, row1, row2, row3), (low0, low1, low2, low3)
    mix_end = 2 * width
    mix_copy = copies.start(rest_hbm.at[:, :mix_end], mix)
    row_copies = [copies.start(p, rows.at[block(k)]) for k, p in enumerate(row_pieces)]
    down_copy = copies.start(rest_hbm.at[:, mix_end : mix_end + width], down)
    low_copies = [copies.start(p, low.at[block(k)]) for k, p in enumerate(low_pieces)]
    for r in (1, 3, 2, 0):
        here = block(r)
        if r == 1:
            copies.finish([mix_copy])
        copies.finish([row_copies[r]])
        copies.start(rows.at[here], rows_hbm.at[here])
        gained = (rows[here, :].astype(F32) * row_gain_ref[1:2, :]).astype(BF16)
        gate_up = nn(gained, mix[...])
        gate, up = gate_up[:, :width], gate_up[:, width:]
        sigmoid = 1.0 / (1.0 + jnp.exp(-gate))
        silu = gate * sigmoid
        active[here, :] = (silu * up).astype(BF16)
        if r == 1:
            copies.finish([down_copy])
        copies.finish([low_copies[r]])
        copies.start(low.at[here], low_hbm.at[here])
        act_grad = nn(low[here, :], down[...])
        gate_low = (act_grad * up * (sigmoid + silu * (1.0 - sigmoid))).astype(BF16)
        up_low = (act_grad * silu).astype(BF16)
        grads[here, :width] = gate_low
        grads[here, width:] = up_low
        partial[r] = nt(grads[here, :], mix[...]).astype(BF16)
        copies.start(partial.at[r], (send_hbm if r % 2 else keep_hbm).at[r // 2])
        copies.start(grads.at[here], grads_hbm.at[here])
        copies.start(active.at[here], active_hbm.at[here])
    copies.finish()


def product_kernel(
    left_hbm, weight_hbm, keep_hbm, send_hbm, left, weight, partial, semaphores, *, start
):
    copies = Copies(semaphores)
    weight_copy = copies.start(weight_hbm.at[:, start : start + left.shape[1]], weight)
    loads = [copies.start(left_hbm.at[block(r)], left.at[block(r)]) for r in range(GROUP)]
    copies.finish([weight_copy])
    for r in (1, 3, 2, 0):
        copies.finish([loads[r]])
        partial[r] = nt(left[block(r), :], weight[...]).astype(BF16)
        copies.start(partial.at[r], (send_hbm if r % 2 else keep_hbm).at[r // 2])
    copies.finish()


def outer_kernel(*refs, pieces):
    sources, refs = refs[: sum(pieces) + len(pieces)], refs[sum(pieces) + len(pieces) :]
    out_hbm, *scratch, result, semaphores = refs
    copies = Copies(semaphores)
    loads, index = [], 0
    for p, count in enumerate(pieces):
        left, right = scratch[2 * p], scratch[2 * p + 1]
        rows = left.shape[0] // count
        right_copy = copies.start(sources[index + count], right)
        loads.append([])
        for k in range(left.shape[1] // ROWS):
            loads[p].append(
                [
                    copies.start(
                        sources[index + n].at[:, block(k)],
                        left.at[pl.ds(n * rows, rows), block(k)],
                    )
                    for n in range(count)
                ]
            )
        loads[p][0].append(right_copy)
        index += count + 1
    start = 0
    for p in range(len(pieces)):
        left, right = scratch[2 * p], scratch[2 * p + 1]
        columns = slice(start, start + right.shape[1])
        start += right.shape[1]
        for k in range(left.shape[1] // ROWS):
            copies.finish(loads[p][k])
            product = tn(left[:, block(k)], right[...]).astype(BF16)
            for j in range(ROWS // PART):
                result[k * (ROWS // PART) + j, :, columns] = product[j * PART : (j + 1) * PART]
            if p == len(pieces) - 1:
                copies.start(result.at[block_parts(k)], out_hbm.at[block_parts(k)])
    copies.finish()


def block_parts(index):
    return pl.ds(index * (ROWS // PART), ROWS // PART)


def backward_kernel(
    place_ref,
    piece0,
    piece1,
    piece2,
    piece3,
    out_hbm,
    attended_hbm,
    queries_hbm,
    keys_hbm,
    values_hbm,
    query_hat_hbm,
    key_hat_hbm,
    inverse_hbm,
    cosine_hbm,
    sine_hbm,
    first_hbm,
    gain_ref,
    query0,
    query1,
    query2,
    query3,
    pair0,
    pair1,
    pair2,
    pair3,
    keep_hbm,
    send_hbm,
    rows,
    w_out,
    attended,
    queries,
    keys,
    values,
    query_hat,
    key_hat,
    inverse,
    cosine,
    sine,
    grads,
    key_grad,
    value_grad,
    query_grad,
    in_low,
    first_rows,
    query_result,
    pair_result,
    w_in,
    partial,
    semaphores,
):
    me = place_ref[0]
    copies = Copies(semaphores)
    pieces = (piece0, piece1, piece2, piece3)
    in_width = in_low.shape[1]
    out_copy = copies.start(out_hbm.at[:, in_width : in_width + Q_WIDTH], w_out)
    piece_copies = [copies.start(p, rows.at[block(k)]) for k, p in enumerate(pieces)]
    attended_copy = copies.start(attended_hbm, attended)
    middle = [
        copies.start(source, target)
        for source, target in (
            (queries_hbm, queries),
            (keys_hbm, keys),
            (values_hbm, values),
        )
    ]
    late = [
        copies.start(source, target)
        for source, target in (
            (query_hat_hbm, query_hat),
            (key_hat_hbm, key_hat),
            (inverse_hbm, inverse),
            (cosine_hbm, cosine),
            (sine_hbm, sine),
        )
    ]
    first_copy = copies.start(first_hbm, first_rows)
    in_copy = copies.start(out_hbm.at[:, :in_width], w_in)
    lane = lanes_of((ROWS, HD))
    copies.finish([out_copy])
    for r in range(GROUP):
        there = dynamic_block(me ^ r)
        copies.finish([piece_copies[r]])
        grad = nn(rows[block(r), :], w_out[...]).astype(BF16)
        if r == 0:
            copies.finish([attended_copy])
        products = grad.astype(F32) * attended[block(r), :].astype(F32)
        for h in range(HEADS):
            columns = slice(h * HD, (h + 1) * HD)
            delta = jnp.sum(products[:, columns], axis=1, keepdims=True)
            extra = jnp.zeros((ROWS, HD), BF16)
            for k, term in enumerate(three_terms(-jnp.broadcast_to(delta, (ROWS, HD)))):
                extra = jnp.where(lane == k, term, extra)
            grads[h, there, :HD] = grad[:, columns]
            grads[h, there, HD:] = extra
    copies.finish(middle)
    causal = lax.broadcasted_iota(jnp.int32, (ROWS, ROWS), 0) <= lax.broadcasted_iota(
        jnp.int32, (ROWS, ROWS), 1
    )
    causal = jnp.concatenate([causal] * (HEADS // KV), axis=1)
    for g in range(KV):
        for kb in range(GROUP):
            key, value = keys[g, block(kb), :], values[g, block(kb), :]
            key_sum, value_sum = None, None
            for rb in range(kb, GROUP):
                both = queries[2 * g : 2 * g + 2, block(rb), :].reshape(2 * ROWS, 2 * HD)
                both_grad = grads[2 * g : 2 * g + 2, block(rb), :].reshape(2 * ROWS, 2 * HD)
                probs = jnp.exp2(nt(key, both))
                if rb == kb:
                    probs = jnp.where(causal, probs, 0.0)
                score_grad = (probs * nt(value, both_grad)).astype(BF16)
                value_part = nn(probs.astype(BF16), both_grad[:, :HD])
                key_part = nn(score_grad, both[:, :HD])
                value_sum = value_part if value_sum is None else value_sum + value_part
                key_sum = key_part if key_sum is None else key_sum + key_part
                query_part = tn(key[:, :HD], score_grad)
                if kb == 0:
                    query_grad[g, rb] = query_part
                else:
                    query_grad[g, rb] += query_part
            key_grad[g, block(kb), :] = key_sum * (1.0 / LOG2E)
            value_grad[g, block(kb), :] = value_sum
    copies.finish(late)
    gains = (gain_ref[0:1, :], gain_ref[1:2, :])
    sums = [jnp.zeros((1, HD), F32), jnp.zeros((1, HD), F32)]
    for i in range(GROUP):
        here = block(i)
        there = me ^ i
        cos, sin = cosine[here, :], sine[here, :]
        parts = []
        for j in range(HEADS + KV):
            kind = 0 if j < HEADS else 1
            if kind == 0:
                g, hh = j // 2, j % 2
                turned = query_grad[g, i, :, hh * ROWS : (hh + 1) * ROWS].T * SCALE
                hat = query_hat[here, j * HD : (j + 1) * HD].astype(F32)
            else:
                g = j - HEADS
                turned = key_grad[g, here, :]
                hat = key_hat[here, g * HD : (g + 1) * HD].astype(F32)
            gradient = turned * cos - turn(turned) * sin
            sums[kind] = sums[kind] + jnp.sum(gradient * hat, axis=0, keepdims=True)
            gained = gradient * gains[kind]
            parts.append(
                (
                    inverse[here, j : j + 1]
                    * (gained - hat * jnp.mean(gained * hat, axis=1, keepdims=True))
                ).astype(BF16)
            )
        for g in range(KV):
            parts.append(value_grad[g, here, :].astype(BF16))
        low = jnp.concatenate(parts, axis=1)
        in_low[dynamic_block(there), :] = low
        if i == 0:
            copies.finish([in_copy])
        partial[i] = nt(low, w_in[...]).astype(BF16)
        copies.start_choice(partial.at[i], keep_hbm, send_hbm, there)
    sums = jnp.concatenate(sums, axis=0)
    high = sums.astype(BF16).astype(F32)
    riders = [high, sums - high, jnp.zeros((PART // X - 4, HD), F32)] * X
    riders = jnp.concatenate(riders, axis=0).astype(BF16)
    copies.finish([first_copy])
    pair_width = in_width - Q_WIDTH
    pair_outs = (pair0, pair1, pair2, pair3)
    for z in range(Z):
        product = tn(first_rows[:, block(z)], in_low[:, Q_WIDTH:]).astype(BF16)
        for y in range(Y):
            k = lax.rem(y + 4 - place_ref[2], 4)
            part = pl.ds(z * PART, PART)
            pair_result[k, part, :pair_width] = product[y * PART : (y + 1) * PART]
            pair_result[k, part, pair_width:] = riders
    for k in (2, 1, 3, 0):
        copies.start(pair_result.at[k], pair_outs[k])
    query_outs = (query0, query1, query2, query3)
    for k in (2, 1, 3, 0):
        z = lax.rem(place_ref[1] + k, 4)
        columns = pl.ds(pl.multiple_of(z * ROWS, ROWS), ROWS)
        query_result[k] = tn(first_rows[:, columns], in_low[:, :Q_WIDTH]).astype(BF16)
        copies.start(query_result.at[k], query_outs[k])
    copies.finish()


def shaped(shape, dtype=BF16):
    return jax.ShapeDtypeStruct(shape, dtype)


def call(kernel, operands, results, scratch, copies, cost, small=None, free=(), weight=1.0):
    in_specs = [pl.BlockSpec(memory_space=pltpu.HBM)] * len(operands)
    chosen = {0: pltpu.SMEM} if small is None else small
    for index, space in chosen.items():
        in_specs[index] = pl.BlockSpec(memory_space=space)
    for index in free:
        in_specs[index] = pl.BlockSpec(memory_space=pl.ANY)
    out_specs = [pl.BlockSpec(memory_space=pltpu.HBM)] * len(results)
    operands = [
        x if index in chosen or index in free else pltpu.with_memory_space_constraint(x, pltpu.HBM)
        for index, x in enumerate(operands)
    ]
    flops, transcendentals = cost
    moved = sum(math.prod(a.shape) * a.dtype.itemsize for a in (*operands, *results))
    return pl.pallas_call(
        kernel,
        out_shape=[pltpu.HBM(r.shape, r.dtype) for r in results],
        in_specs=in_specs,
        out_specs=out_specs,
        scratch_shapes=[pltpu.VMEM(s, d) for s, d in scratch]
        + [pltpu.SemaphoreType.DMA((copies,))],
        compiler_params=pltpu.CompilerParams(vmem_limit_bytes=40 * MIB),
        cost_estimate=pl.CostEstimate(
            flops=int(flops * weight),
            bytes_accessed=int(moved * weight),
            transcendentals=int(transcendentals * weight),
        ),
    )(*operands)


def product(left, weight, start=0):
    (tree, depth), width = left.shape, weight.shape[0]
    pair = shaped((2, ROWS, width))
    return call(
        functools.partial(product_kernel, start=start),
        (left, weight),
        (pair, pair),
        (((tree, depth), BF16), ((width, depth), BF16), ((GROUP, ROWS, width), BF16)),
        1 + 2 * GROUP,
        (2 * tree * depth * width, 0),
        small={},
        weight=0.05,
    )


def outer(*pairs):
    pairs = [(left if isinstance(left, tuple) else (left,), right) for left, right in pairs]
    operands = [a for left, right in pairs for a in (*left, right)]
    tree, width = pairs[0][1].shape[0], sum(right.shape[1] for _, right in pairs)
    depth = pairs[0][0][0].shape[1]
    result = (depth // PART, PART, width)
    scratch = [((tree, a.shape[1]), BF16) for left, right in pairs for a in (left[0], right)]
    pieces = tuple(len(left) for left, _ in pairs)
    return call(
        functools.partial(outer_kernel, pieces=pieces),
        operands,
        (shaped(result),),
        scratch + [(result, BF16)],
        (sum(pieces) + 1) * (depth // ROWS) + len(pieces),
        (2 * tree * depth * width, 0),
        small={},
        free=tuple(range(4)) if pieces == (4,) else (),
        weight=0.05,
    )[0]


def local(
    layer_input,
    cotangent,
    parents,
    offsets,
    w_query,
    w_key,
    w_value,
    w_output,
    w_gate,
    w_up,
    w_down,
    norm_attn,
    norm_mlp,
    query_gain,
    key_gain,
):
    tree = GROUP * ROWS
    width = layer_input.shape[1]
    ff_width = w_gate.shape[1]
    in_width = Q_WIDTH + 2 * K_WIDTH
    fsdp_index = lax.axis_index("fsdp")
    place = jnp.stack([lax.axis_index("tp"), fsdp_index // (Y * X), fsdp_index // X % Y])
    place = place.astype(jnp.int32)

    gains = gather_small(jnp.stack([norm_attn, norm_mlp]))
    gain_attn, gain_mlp = gains[0][:, None], gains[1][:, None]
    w_early = jnp.concatenate([w_query, w_key, w_value, w_output.T], axis=1)
    early_other, gains = lax.optimization_barrier((swapped(w_early), gains))
    early = gather_plane(in_order(w_early, early_other))
    row_gains = gather_gains(gains)
    w_late = jnp.concatenate([w_gate, w_up, w_down.T], axis=1)
    w_late, row_gains = lax.optimization_barrier((w_late, row_gains))
    late = gather_plane(in_order(w_late, swapped(w_late)))
    row_gains = jnp.pad(row_gains, ((0, 6), (0, 0)))

    inverse_one = lax.rsqrt(jnp.mean(layer_input * layer_input, axis=1, keepdims=True) + EPSILON)
    normed_one = layer_input * inverse_one
    first_low, _ = lax.optimization_barrier((normed_one.astype(BF16), early_other))
    first_pieces = gather_rows(first_low)
    out_low, _ = lax.optimization_barrier((cotangent.astype(BF16), first_pieces[2]))
    low_pieces = gather_rows(out_low)

    row_ancestry, member, path_position = tree_tables(parents[0], offsets[0], tree)
    cosine, sine = rotary(path_position)
    query_extra, key_extra = score_terms(row_ancestry, member)
    head_gains = jnp.pad(jnp.stack([query_gain, key_gain]), ((0, 6), (0, 0)))
    first_pieces, low_pieces, cosine, sine, query_extra, key_extra = lax.optimization_barrier(
        (first_pieces, low_pieces, cosine, sine, query_extra, key_extra)
    )

    pair_shape = (2, ROWS, width)
    attention_flops = 2 * tree * tree * HD * HEADS
    (
        queries,
        keys,
        values,
        attended,
        query_hat,
        key_hat,
        inverse,
        first_rows,
        keep,
        send,
    ) = call(
        attention_kernel,
        (
            place,
            *first_pieces,
            early,
            cosine,
            sine,
            query_extra,
            key_extra,
            head_gains,
            row_gains,
        ),
        (
            shaped((HEADS, tree, 2 * HD)),
            shaped((KV, tree, 2 * HD)),
            shaped((KV, tree, 2 * HD)),
            shaped((tree, Q_WIDTH)),
            shaped((tree, Q_WIDTH)),
            shaped((tree, K_WIDTH)),
            shaped((tree, HD), F32),
            shaped((tree, width)),
            shaped(pair_shape),
            shaped(pair_shape),
        ),
        (
            ((tree, width), BF16),
            ((width, in_width), BF16),
            ((width, Q_WIDTH), BF16),
            ((tree, HD), F32),
            ((tree, HD), F32),
            ((tree, HD), BF16),
            ((tree, HD), BF16),
            ((HEADS, tree, 2 * HD), BF16),
            ((KV, tree, 2 * HD), BF16),
            ((KV, tree, 2 * HD), BF16),
            ((tree, Q_WIDTH), BF16),
            ((tree, Q_WIDTH), BF16),
            ((tree, K_WIDTH), BF16),
            ((tree, HD), F32),
            ((GROUP, ROWS, width), BF16),
        ),
        2 + 4 + 4 + 4 + GROUP * (5 + HEADS + 2 * KV),
        (2 * tree * width * (in_width + Q_WIDTH) + 4 * attention_flops, HEADS * tree * tree),
        small={0: pltpu.SMEM, 10: pltpu.VMEM, 11: pltpu.VMEM},
        free=(1, 2, 3, 4),
    )
    mid_rows = layer_input + scatter_rows(keep, send)
    inverse_two = lax.rsqrt(jnp.mean(mid_rows * mid_rows, axis=1, keepdims=True) + EPSILON)
    normed_two = mid_rows * inverse_two
    second_pieces = gather_rows(normed_two.astype(BF16))
    second_rows, out_low, activated, gate_up_low, grad_keep, grad_send = call(
        mlp_kernel,
        (*second_pieces, *low_pieces, late, row_gains),
        (
            shaped((tree, width)),
            shaped((tree, width)),
            shaped((tree, ff_width)),
            shaped((tree, 2 * ff_width)),
            shaped(pair_shape),
            shaped(pair_shape),
        ),
        (
            ((tree, width), BF16),
            ((tree, width), BF16),
            ((width, 2 * ff_width), BF16),
            ((width, ff_width), BF16),
            ((tree, ff_width), BF16),
            ((tree, 2 * ff_width), BF16),
            ((GROUP, ROWS, width), BF16),
        ),
        2 + 4 * GROUP + 3 * GROUP,
        (10 * tree * width * ff_width, tree * ff_width),
        small={9: pltpu.VMEM},
        free=(0, 1, 2, 3),
    )
    grad_own, grad_other = add_cores(grad_keep, lax.ppermute(grad_send, "tp", flip(1)))
    grad_other = lax.ppermute(grad_other, "tp", flip(2))
    mlp_blocks = outer((second_rows, gate_up_low), (out_low, activated))
    grad_other, _ = lax.optimization_barrier((grad_other, mlp_blocks))
    mlp_sums = scatter_plane(mlp_blocks.reshape(width, 3 * ff_width))
    second_grad = grad_own + grad_other.astype(F32)
    mid_grad = cotangent + norm_back(
        second_grad * row_gains[1:2], normed_two, inverse_two
    )
    mid_low = mid_grad.astype(BF16)
    across = lax.ppermute(mid_low, "tp", flip(2))
    beside = lax.ppermute(mid_low, "tp", flip(1))
    out_keep, out_send = product(activated, late, 2 * ff_width)
    across, out_keep, out_send = lax.optimization_barrier((across, out_keep, out_send))
    mid_pieces = (mid_low, beside, across, lax.ppermute(across, "tp", flip(1)))
    out_send = lax.ppermute(out_send, "tp", flip(1))
    out_blocks, mid_pieces = lax.optimization_barrier(
        (outer((tuple(mid_pieces), attended)), tuple(mid_pieces))
    )
    out_blocks = exchange_plane(out_blocks)
    *in_blocks, first_keep, first_send = call(
        backward_kernel,
        (
            place,
            *mid_pieces,
            early,
            attended,
            queries,
            keys,
            values,
            query_hat,
            key_hat,
            inverse,
            cosine,
            sine,
            first_rows,
            head_gains,
        ),
        (
            *(shaped((ROWS, Q_WIDTH)),) * 4,
            *(shaped((ROWS, 2 * K_WIDTH + HD)),) * 4,
            shaped(pair_shape),
            shaped(pair_shape),
        ),
        (
            ((tree, width), BF16),
            ((width, Q_WIDTH), BF16),
            ((tree, Q_WIDTH), BF16),
            ((HEADS, tree, 2 * HD), BF16),
            ((KV, tree, 2 * HD), BF16),
            ((KV, tree, 2 * HD), BF16),
            ((tree, Q_WIDTH), BF16),
            ((tree, K_WIDTH), BF16),
            ((tree, HD), F32),
            ((tree, HD), F32),
            ((tree, HD), F32),
            ((HEADS, tree, 2 * HD), BF16),
            ((KV, tree, HD), F32),
            ((KV, tree, HD), F32),
            ((KV, GROUP, HD, 2 * ROWS), F32),
            ((tree, in_width), BF16),
            ((tree, width), BF16),
            ((4, ROWS, Q_WIDTH), BF16),
            ((4, ROWS, 2 * K_WIDTH + HD), BF16),
            ((width, in_width), BF16),
            ((GROUP, ROWS, width), BF16),
        ),
        1 + 4 + 1 + 3 + 5 + 2 + GROUP + 8,
        (2 * tree * width * (Q_WIDTH + 2 * in_width) + 7 * attention_flops, HEADS * tree * tree),
        small={0: pltpu.SMEM, 16: pltpu.VMEM},
        free=(1, 2, 3, 4),
        weight=3.0,
    )
    out_shard = scatter_pair(jnp.sum(out_blocks.astype(F32), axis=0))
    in_blocks, out_keep, out_send, out_blocks = lax.optimization_barrier(
        (in_blocks, out_keep, out_send, out_blocks)
    )
    first_grad = scatter_rows(first_keep, first_send)
    layer_output = mid_rows + scatter_chips(*add_cores(out_keep, out_send))
    query_sum = scatter_line(add_line(send_line(in_blocks[:4], "z")), "y")
    pair_sum = scatter_line(add_line(send_line(in_blocks[4:], "y")), "z")
    mlp_shard = scatter_pair(mlp_sums)
    in_shard = scatter_pair(jnp.concatenate([query_sum, pair_sum], axis=1))
    gain_rows = in_shard[:4, in_width:]
    gain_row = (gain_rows[:2] + gain_rows[2:]).reshape(2 * HD)
    in_shard = in_shard[:, :in_width]
    mix_shard, down_shard = mlp_shard[:, : 2 * ff_width], mlp_shard[:, 2 * ff_width :]
    input_grad = mid_grad + norm_back(first_grad * row_gains[0:1], normed_one, inverse_one)

    def products(weight, shard):
        return jnp.sum(weight.astype(F32) * shard, axis=1)

    query_shard = in_shard[:, :Q_WIDTH]
    key_shard = in_shard[:, Q_WIDTH : Q_WIDTH + K_WIDTH]
    value_shard = in_shard[:, Q_WIDTH + K_WIDTH :]
    gate_shard, up_shard = mix_shard[:, :ff_width], mix_shard[:, ff_width:]
    attn_part = (
        products(w_query, query_shard)
        + products(w_key, key_shard)
        + products(w_value, value_shard)
    )
    mlp_part = products(w_gate, gate_shard) + products(w_up, up_shard)
    sums = sum_group(jnp.concatenate([gain_row, attn_part, mlp_part]))
    own = lax.axis_index("tp") * norm_attn.shape[0]
    norm_attn_grad = lax.dynamic_slice_in_dim(sums, 2 * HD + own, norm_attn.shape[0])
    norm_mlp_grad = lax.dynamic_slice_in_dim(
        sums, 2 * HD + attn_part.shape[0] + own, norm_mlp.shape[0]
    )
    return (
        layer_output,
        input_grad,
        query_shard * gain_attn,
        key_shard * gain_attn,
        value_shard * gain_attn,
        out_shard.T,
        gate_shard * gain_mlp,
        up_shard * gain_mlp,
        down_shard.T,
        norm_attn_grad,
        norm_mlp_grad,
        sums[:HD],
        sums[HD : 2 * HD],
    )


def solution(mesh):
    in_specs = (
        P(("fsdp", "tp"), None),
        P(("fsdp", "tp"), None),
        P("fsdp", None),
        P("fsdp", None),
        P("fsdp", "tp"),
        P("fsdp", "tp"),
        P("fsdp", "tp"),
        P("tp", "fsdp"),
        P("fsdp", "tp"),
        P("fsdp", "tp"),
        P("tp", "fsdp"),
        P(("fsdp", "tp")),
        P(("fsdp", "tp")),
        P(),
        P(),
    )
    out_specs = (
        P(("fsdp", "tp"), None),
        P(("fsdp", "tp"), None),
        P("fsdp", "tp"),
        P("fsdp", "tp"),
        P("fsdp", "tp"),
        P("tp", "fsdp"),
        P("fsdp", "tp"),
        P("fsdp", "tp"),
        P("tp", "fsdp"),
        P(("fsdp", "tp")),
        P(("fsdp", "tp")),
        P(),
        P(),
    )
    return jax.shard_map(local, mesh=mesh, in_specs=in_specs, out_specs=out_specs, check_vma=False)
```

```python
import functools
import math

import jax
import jax.numpy as jnp
from jax import lax
from jax.experimental import pallas as pl
from jax.experimental.pallas import tpu as pltpu
from jax.sharding import PartitionSpec as P

H = 16
KVH = 8
HD = 128
GROUP = 4
ROWS = 256
HEADS = H // GROUP
Z, Y, X = 4, 4, 2
PART = 64
KV = KVH // GROUP
Q_WIDTH = HEADS * HD
K_WIDTH = KV * HD

EPSILON = 1e-06
THETA = 1000000.0
BARRED = -512.0
LOG2E = 1.0 / math.log(2.0)
SCALE = 1.0 / math.sqrt(HD)
MIB = 1024 * 1024
BF16 = jnp.bfloat16
F32 = jnp.float32


def tree_tables(parents, offsets, tree_rows):
    positions = jnp.arange(tree_rows, dtype=jnp.int32)
    labels = jnp.arange(parents.shape[0], dtype=jnp.int32)
    segment = jnp.sum((positions[:, None] >= offsets[None, 1:]).astype(jnp.int32), axis=1)
    member = segment[:, None] == labels[None, :]
    parent_pick = parents[:, None] == labels[None, :]
    grandparent = jnp.sum(jnp.where(parent_pick, parents[None, :], 0), axis=1)
    ancestry = (
        (labels[None, :] == labels[:, None])
        | (labels[None, :] == parents[:, None])
        | (labels[None, :] == grandparent[:, None])
    )
    segment_ends = jnp.concatenate([offsets[1:], jnp.full((1,), tree_rows, jnp.int32)])
    lengths = segment_ends - offsets
    parent_len = jnp.sum(jnp.where(parent_pick, lengths[None, :], 0), axis=1)
    grand_pick = grandparent[:, None] == labels[None, :]
    grand_len = jnp.sum(jnp.where(grand_pick, lengths[None, :], 0), axis=1)
    path_start = jnp.where(labels > 0, parent_len, 0) + jnp.where(parents > 0, grand_len, 0)
    path_position = positions + jnp.sum(
        jnp.where(member, (path_start - offsets)[None, :], 0), axis=1
    )
    member_float = member.astype(F32)
    row_ancestry = jnp.dot(member_float, ancestry.astype(F32), preferred_element_type=F32)
    return (row_ancestry, member_float, path_position)


def score_terms(row_ancestry, member):
    spare = HD - member.shape[1]
    query_extra = jnp.pad((1.0 - row_ancestry) * BARRED, ((0, 0), (0, spare)))
    column = jnp.arange(HD, dtype=jnp.int32)[None, :]
    key_extra = jnp.pad(member, ((0, 0), (0, spare)))
    key_extra = jnp.where((column >= 8) & (column <= 10), 1.0, key_extra)
    return query_extra.astype(BF16), key_extra.astype(BF16)


def rotary(path_position):
    frequency = jnp.exp(jnp.arange(0, HD, 2).astype(F32) * (-math.log(THETA) / HD))
    angles = path_position.astype(F32)[:, None] * frequency[None, :]
    cosine, sine = jnp.cos(angles), jnp.sin(angles)
    return jnp.concatenate([cosine, cosine], axis=1), jnp.concatenate([-sine, sine], axis=1)


def norm_back(gradient, normed, inverse):
    return inverse * (gradient - normed * jnp.mean(gradient * normed, axis=-1, keepdims=True))


def flip(bits):
    return [(t, t ^ bits) for t in range(GROUP)]


def swap_x():
    return [(f, f ^ 1) for f in range(Z * Y * X)]


def planes():
    return [[(z * Y + y) * X + x for z in range(Z) for y in range(Y)] for x in range(X)]


def swapped(value):
    return lax.ppermute(value, "fsdp", swap_x())


def in_order(own, other):
    second = lax.axis_index("fsdp") % X == 1
    return jnp.concatenate(
        [jnp.where(second, other, own), jnp.where(second, own, other)], axis=0
    )


def gather_plane(pair):
    return lax.all_gather(pair, "fsdp", axis=0, tiled=True, axis_index_groups=planes())


def scatter_plane(partial):
    return lax.psum_scatter(
        partial, "fsdp", scatter_dimension=0, tiled=True, axis_index_groups=planes()
    )


def line(dim, step):
    pairs = []
    for z in range(Z):
        for y in range(Y):
            for x in range(X):
                far_z = (z + step) % Z if dim == "z" else z
                far_y = (y + step) % Y if dim == "y" else y
                pairs.append(((z * Y + y) * X + x, (far_z * Y + far_y) * X + x))
    return pairs


def lines(dim):
    if dim == "z":
        return [[(z * Y + y) * X + x for z in range(Z)] for y in range(Y) for x in range(X)]
    return [[(z * Y + y) * X + x for y in range(Y)] for z in range(Z) for x in range(X)]


def send_line(blocks, dim):
    return [blocks[0]] + [
        lax.ppermute(blocks[k], "fsdp", line(dim, k)) for k in range(1, 4)
    ]


def add_line(blocks):
    return sum(block.astype(F32) for block in blocks).astype(BF16)


def scatter_line(total, dim):
    parts = total.reshape(4, -1, total.shape[1])
    parts = lax.all_to_all(parts, "fsdp", 0, 0, tiled=True, axis_index_groups=lines(dim))
    return jnp.sum(parts.astype(F32), axis=0)


def exchange_plane(blocks):
    return lax.all_to_all(blocks, "fsdp", 0, 0, tiled=True, axis_index_groups=planes())


def scatter_pair(total):
    here = lax.axis_index("fsdp") % X
    halves = total.reshape(X, -1, total.shape[1])
    keep = lax.dynamic_index_in_dim(halves, here, 0, keepdims=False)
    send = lax.dynamic_index_in_dim(halves, 1 - here, 0, keepdims=False)
    return keep.astype(F32) + swapped(send.astype(BF16)).astype(F32)


def gather_rows(rows):
    across = lax.ppermute(rows, "tp", flip(2))
    beside = lax.ppermute(rows, "tp", flip(1))
    far = lax.ppermute(across, "tp", flip(1))
    return rows, beside, across, far


def add_cores(keep, received):
    other = (keep[1].astype(F32) + received[1].astype(F32)).astype(BF16)
    other, keep, received = lax.optimization_barrier((other, keep, received))
    return keep[0].astype(F32) + received[0].astype(F32), other


def scatter_chips(own, other):
    return own + lax.ppermute(other, "tp", flip(2)).astype(F32)


def scatter_rows(keep, send):
    return scatter_chips(*add_cores(keep, lax.ppermute(send, "tp", flip(1))))


def gather_small(values):
    me = lax.axis_index("tp")
    total = jnp.zeros((GROUP,) + values.shape, values.dtype)
    for bits in range(GROUP):
        piece = values if bits == 0 else lax.ppermute(values, "tp", flip(bits))
        total = lax.dynamic_update_index_in_dim(total, piece, me ^ bits, 0)
    return jnp.swapaxes(total, 0, 1).reshape(values.shape[0], -1)


def gather_gains(values):
    fsdp = lax.axis_size("fsdp")
    copies = jnp.broadcast_to(values.reshape(1, 1, -1), (fsdp, 1, values.size))
    full = lax.all_to_all(copies, "fsdp", 0, 0, tiled=True)
    full = full.reshape(fsdp, *values.shape)
    return jnp.swapaxes(full, 0, 1).reshape(values.shape[0], -1)


def sum_group(values):
    return values + sum(lax.ppermute(values, "tp", flip(bits)) for bits in range(1, GROUP))


def nn(left, right):
    return lax.dot_general(left, right, (((1,), (0,)), ((), ())), preferred_element_type=F32)


def nt(left, right):
    return lax.dot_general(left, right, (((1,), (1,)), ((), ())), preferred_element_type=F32)


def tn(left, right):
    return lax.dot_general(left, right, (((0,), (0,)), ((), ())), preferred_element_type=F32)


def block(index):
    return pl.ds(index * ROWS, ROWS)


def dynamic_block(index):
    return pl.ds(pl.multiple_of(index * ROWS, ROWS), ROWS)


def three_terms(value):
    high = value.astype(BF16)
    rest = value - high.astype(F32)
    middle = rest.astype(BF16)
    return high, middle, (rest - middle.astype(F32)).astype(BF16)


def lanes_of(shape):
    return lax.broadcasted_iota(jnp.int32, shape, 1)


class Copies:
    def __init__(self, semaphores):
        self.semaphores, self.used, self.open = semaphores, 0, []

    def start(self, source, target):
        copy = pltpu.make_async_copy(source, target, self.semaphores.at[self.used])
        self.used += 1
        copy.start()
        self.open.append(copy)
        return copy

    def start_choice(self, source, evens, odds, index):
        semaphore = self.semaphores.at[self.used]
        self.used += 1
        for bit, target in ((0, evens), (1, odds)):

            @pl.when(index % 2 == bit)
            def _():
                pltpu.make_async_copy(source, target.at[index // 2], semaphore).start()

        self.open.append(pltpu.make_async_copy(source, evens.at[0], semaphore))

    def finish(self, copies=None):
        for copy in list(self.open) if copies is None else copies:
            copy.wait()
            self.open = [other for other in self.open if other is not copy]


def turn(rows):
    return pltpu.roll(rows, HD // 2, 1)


def attention_kernel(
    place_ref,
    piece0,
    piece1,
    piece2,
    piece3,
    in_hbm,
    cosine_hbm,
    sine_hbm,
    query_extra_hbm,
    key_extra_hbm,
    gain_ref,
    row_gain_ref,
    queries_hbm,
    keys_hbm,
    values_hbm,
    attended_hbm,
    query_hat_hbm,
    key_hat_hbm,
    inverse_hbm,
    rows_hbm,
    keep_hbm,
    send_hbm,
    rows,
    w_in,
    w_out,
    cosine,
    sine,
    query_extra,
    key_extra,
    queries,
    keys,
    values,
    attended,
    query_hat,
    key_hat,
    inverse,
    partial,
    semaphores,
):
    me = place_ref[0]
    copies = Copies(semaphores)
    pieces = (piece0, piece1, piece2, piece3)
    in_width = w_in.shape[1]
    first = [copies.start(in_hbm.at[:, :in_width], w_in)]
    for bits, piece in enumerate(pieces):
        first.append(copies.start(piece, rows.at[dynamic_block(me ^ bits)]))
    for source, target in (
        (cosine_hbm, cosine),
        (sine_hbm, sine),
        (query_extra_hbm, query_extra),
        (key_extra_hbm, key_extra),
    ):
        first.append(copies.start(source, target))
    out_copy = copies.start(in_hbm.at[:, in_width : in_width + Q_WIDTH], w_out)
    copies.finish(first)
    for bits in range(GROUP):
        copies.start(rows.at[dynamic_block(me ^ bits)], rows_hbm.at[block(bits)])
    query_gain = gain_ref[0:1, :] * (SCALE * LOG2E)
    key_gain = gain_ref[1:2, :]
    lane = lanes_of((ROWS, HD))
    for g in range(KV):
        values[g, :, HD:] = jnp.ones((GROUP * ROWS, HD), BF16)
        keys[g, :, HD:] = key_extra[...]
    causal = lax.broadcasted_iota(jnp.int32, (ROWS, ROWS), 0) >= lax.broadcasted_iota(
        jnp.int32, (ROWS, ROWS), 1
    )
    causal = jnp.concatenate([causal] * (HEADS // KV), axis=0)

    for i in range(GROUP):
        here = block(i)
        there = me ^ i
        gained = (rows[here, :].astype(F32) * row_gain_ref[0:1, :]).astype(BF16)
        projected = nn(gained, w_in[...])
        cos, sin = cosine[here, :], sine[here, :]
        inverses = jnp.zeros((ROWS, HD), F32)
        for j in range(HEADS + KV):
            raw = projected[:, j * HD : (j + 1) * HD]
            scale = lax.rsqrt(jnp.mean(raw * raw, axis=1, keepdims=True) + EPSILON)
            inverses = jnp.where(lane == j, scale, inverses)
            hat = raw * scale
            gained = hat * (query_gain if j < HEADS else key_gain)
            roped = (gained * cos + turn(gained) * sin).astype(BF16)
            if j < HEADS:
                query_hat[here, j * HD : (j + 1) * HD] = hat.astype(BF16)
                queries[j, here, :HD] = roped
                queries[j, here, HD:] = query_extra[here, :]
            else:
                g = j - HEADS
                key_hat[here, g * HD : (g + 1) * HD] = hat.astype(BF16)
                keys[g, here, :HD] = roped
        inverse[here, :] = inverses
        for g in range(KV):
            start = Q_WIDTH + K_WIDTH + g * HD
            values[g, here, :HD] = projected[:, start : start + HD].astype(BF16)
        parts = []
        for g in range(KV):
            both = queries[2 * g : 2 * g + 2, here, :].reshape(2 * ROWS, 2 * HD)
            mixed = None
            for kb in range(i + 1):
                weights = jnp.exp2(nt(both, keys[g, block(kb), :]))
                if kb == i:
                    weights = jnp.where(causal, weights, 0.0)
                part = nn(weights.astype(BF16), values[g, block(kb), :])
                mixed = part if mixed is None else mixed + part
            total = mixed[:, HD:]
            out = (mixed[:, :HD] / total).astype(BF16)
            logs = three_terms(-jnp.log2(total))
            for hh in range(2):
                h = 2 * g + hh
                parts.append(out[hh * ROWS : (hh + 1) * ROWS])
                extra = queries[h, here, HD:]
                for k, term in enumerate(logs):
                    extra = jnp.where(lane == 8 + k, term[hh * ROWS : (hh + 1) * ROWS], extra)
                queries[h, here, HD:] = extra
        mixed_rows = jnp.concatenate(parts, axis=1)
        attended[here, :] = mixed_rows
        if i == 0:
            copies.finish([out_copy])
        partial[i] = nt(mixed_rows, w_out[...]).astype(BF16)
        copies.start_choice(partial.at[i], keep_hbm, send_hbm, there)
        copies.start(attended.at[here], attended_hbm.at[dynamic_block(there)])
        copies.start(query_hat.at[here], query_hat_hbm.at[here])
        copies.start(key_hat.at[here], key_hat_hbm.at[here])
        copies.start(inverse.at[here], inverse_hbm.at[here])
        for h in range(HEADS):
            copies.start(queries.at[h, here], queries_hbm.at[h, here])
        for g in range(KV):
            copies.start(keys.at[g, here], keys_hbm.at[g, here])
            copies.start(values.at[g, here], values_hbm.at[g, here])
    copies.finish()


def mlp_kernel(
    row0,
    row1,
    row2,
    row3,
    low0,
    low1,
    low2,
    low3,
    rest_hbm,
    row_gain_ref,
    rows_hbm,
    low_hbm,
    active_hbm,
    grads_hbm,
    keep_hbm,
    send_hbm,
    rows,
    low,
    mix,
    down,
    active,
    grads,
    partial,
    semaphores,
):
    copies = Copies(semaphores)
    width = down.shape[1]
    row_pieces, low_pieces = (row0, row1, row2, row3), (low0, low1, low2, low3)
    mix_end = 2 * width
    mix_copy = copies.start(rest_hbm.at[:, :mix_end], mix)
    row_copies = [copies.start(p, rows.at[block(k)]) for k, p in enumerate(row_pieces)]
    down_copy = copies.start(rest_hbm.at[:, mix_end : mix_end + width], down)
    low_copies = [copies.start(p, low.at[block(k)]) for k, p in enumerate(low_pieces)]
    for r in (1, 3, 2, 0):
        here = block(r)
        if r == 1:
            copies.finish([mix_copy])
        copies.finish([row_copies[r]])
        copies.start(rows.at[here], rows_hbm.at[here])
        gained = (rows[here, :].astype(F32) * row_gain_ref[1:2, :]).astype(BF16)
        gate_up = nn(gained, mix[...])
        gate, up = gate_up[:, :width], gate_up[:, width:]
        sigmoid = 1.0 / (1.0 + jnp.exp(-gate))
        silu = gate * sigmoid
        active[here, :] = (silu * up).astype(BF16)
        if r == 1:
            copies.finish([down_copy])
        copies.finish([low_copies[r]])
        copies.start(low.at[here], low_hbm.at[here])
        act_grad = nn(low[here, :], down[...])
        gate_low = (act_grad * up * (sigmoid + silu * (1.0 - sigmoid))).astype(BF16)
        up_low = (act_grad * silu).astype(BF16)
        grads[here, :width] = gate_low
        grads[here, width:] = up_low
        partial[r] = nt(grads[here, :], mix[...]).astype(BF16)
        copies.start(partial.at[r], (send_hbm if r % 2 else keep_hbm).at[r // 2])
        copies.start(grads.at[here], grads_hbm.at[here])
        copies.start(active.at[here], active_hbm.at[here])
    copies.finish()


def product_kernel(
    left_hbm, weight_hbm, keep_hbm, send_hbm, left, weight, partial, semaphores, *, start
):
    copies = Copies(semaphores)
    weight_copy = copies.start(weight_hbm.at[:, start : start + left.shape[1]], weight)
    loads = [copies.start(left_hbm.at[block(r)], left.at[block(r)]) for r in range(GROUP)]
    copies.finish([weight_copy])
    for r in (1, 3, 2, 0):
        copies.finish([loads[r]])
        partial[r] = nt(left[block(r), :], weight[...]).astype(BF16)
        copies.start(partial.at[r], (send_hbm if r % 2 else keep_hbm).at[r // 2])
    copies.finish()


def outer_kernel(*refs, pieces):
    sources, refs = refs[: sum(pieces) + len(pieces)], refs[sum(pieces) + len(pieces) :]
    out_hbm, *scratch, result, semaphores = refs
    copies = Copies(semaphores)
    loads, index = [], 0
    for p, count in enumerate(pieces):
        left, right = scratch[2 * p], scratch[2 * p + 1]
        rows = left.shape[0] // count
        right_copy = copies.start(sources[index + count], right)
        loads.append([])
        for k in range(left.shape[1] // ROWS):
            loads[p].append(
                [
                    copies.start(
                        sources[index + n].at[:, block(k)],
                        left.at[pl.ds(n * rows, rows), block(k)],
                    )
                    for n in range(count)
                ]
            )
        loads[p][0].append(right_copy)
        index += count + 1
    start = 0
    for p in range(len(pieces)):
        left, right = scratch[2 * p], scratch[2 * p + 1]
        columns = slice(start, start + right.shape[1])
        start += right.shape[1]
        for k in range(left.shape[1] // ROWS):
            copies.finish(loads[p][k])
            product = tn(left[:, block(k)], right[...]).astype(BF16)
            for j in range(ROWS // PART):
                result[k * (ROWS // PART) + j, :, columns] = product[j * PART : (j + 1) * PART]
            if p == len(pieces) - 1:
                copies.start(result.at[block_parts(k)], out_hbm.at[block_parts(k)])
    copies.finish()


def block_parts(index):
    return pl.ds(index * (ROWS // PART), ROWS // PART)


def backward_kernel(
    place_ref,
    piece0,
    piece1,
    piece2,
    piece3,
    out_hbm,
    attended_hbm,
    queries_hbm,
    keys_hbm,
    values_hbm,
    query_hat_hbm,
    key_hat_hbm,
    inverse_hbm,
    cosine_hbm,
    sine_hbm,
    first_hbm,
    gain_ref,
    query0,
    query1,
    query2,
    query3,
    pair0,
    pair1,
    pair2,
    pair3,
    keep_hbm,
    send_hbm,
    rows,
    w_out,
    attended,
    queries,
    keys,
    values,
    query_hat,
    key_hat,
    inverse,
    cosine,
    sine,
    grads,
    key_grad,
    value_grad,
    query_grad,
    in_low,
    first_rows,
    query_result,
    pair_result,
    w_in,
    partial,
    semaphores,
):
    me = place_ref[0]
    copies = Copies(semaphores)
    pieces = (piece0, piece1, piece2, piece3)
    in_width = in_low.shape[1]
    out_copy = copies.start(out_hbm.at[:, in_width : in_width + Q_WIDTH], w_out)
    piece_copies = [copies.start(p, rows.at[block(k)]) for k, p in enumerate(pieces)]
    attended_copy = copies.start(attended_hbm, attended)
    middle = [
        copies.start(source, target)
        for source, target in (
            (queries_hbm, queries),
            (keys_hbm, keys),
            (values_hbm, values),
        )
    ]
    late = [
        copies.start(source, target)
        for source, target in (
            (query_hat_hbm, query_hat),
            (key_hat_hbm, key_hat),
            (inverse_hbm, inverse),
            (cosine_hbm, cosine),
            (sine_hbm, sine),
        )
    ]
    first_copy = copies.start(first_hbm, first_rows)
    in_copy = copies.start(out_hbm.at[:, :in_width], w_in)
    lane = lanes_of((ROWS, HD))
    copies.finish([out_copy])
    for r in range(GROUP):
        there = dynamic_block(me ^ r)
        copies.finish([piece_copies[r]])
        grad = nn(rows[block(r), :], w_out[...]).astype(BF16)
        if r == 0:
            copies.finish([attended_copy])
        products = grad.astype(F32) * attended[block(r), :].astype(F32)
        for h in range(HEADS):
            columns = slice(h * HD, (h + 1) * HD)
            delta = jnp.sum(products[:, columns], axis=1, keepdims=True)
            extra = jnp.zeros((ROWS, HD), BF16)
            for k, term in enumerate(three_terms(-jnp.broadcast_to(delta, (ROWS, HD)))):
                extra = jnp.where(lane == k, term, extra)
            grads[h, there, :HD] = grad[:, columns]
            grads[h, there, HD:] = extra
    copies.finish(middle)
    causal = lax.broadcasted_iota(jnp.int32, (ROWS, ROWS), 0) <= lax.broadcasted_iota(
        jnp.int32, (ROWS, ROWS), 1
    )
    causal = jnp.concatenate([causal] * (HEADS // KV), axis=1)
    for g in range(KV):
        for kb in range(GROUP):
            key, value = keys[g, block(kb), :], values[g, block(kb), :]
            key_sum, value_sum = None, None
            for rb in range(kb, GROUP):
                both = queries[2 * g : 2 * g + 2, block(rb), :].reshape(2 * ROWS, 2 * HD)
                both_grad = grads[2 * g : 2 * g + 2, block(rb), :].reshape(2 * ROWS, 2 * HD)
                probs = jnp.exp2(nt(key, both))
                if rb == kb:
                    probs = jnp.where(causal, probs, 0.0)
                score_grad = (probs * nt(value, both_grad)).astype(BF16)
                value_part = nn(probs.astype(BF16), both_grad[:, :HD])
                key_part = nn(score_grad, both[:, :HD])
                value_sum = value_part if value_sum is None else value_sum + value_part
                key_sum = key_part if key_sum is None else key_sum + key_part
                query_part = tn(key[:, :HD], score_grad)
                if kb == 0:
                    query_grad[g, rb] = query_part
                else:
                    query_grad[g, rb] += query_part
            key_grad[g, block(kb), :] = key_sum * (1.0 / LOG2E)
            value_grad[g, block(kb), :] = value_sum
    copies.finish(late)
    gains = (gain_ref[0:1, :], gain_ref[1:2, :])
    sums = [jnp.zeros((1, HD), F32), jnp.zeros((1, HD), F32)]
    for i in range(GROUP):
        here = block(i)
        there = me ^ i
        cos, sin = cosine[here, :], sine[here, :]
        parts = []
        for j in range(HEADS + KV):
            kind = 0 if j < HEADS else 1
            if kind == 0:
                g, hh = j // 2, j % 2
                turned = query_grad[g, i, :, hh * ROWS : (hh + 1) * ROWS].T * SCALE
                hat = query_hat[here, j * HD : (j + 1) * HD].astype(F32)
            else:
                g = j - HEADS
                turned = key_grad[g, here, :]
                hat = key_hat[here, g * HD : (g + 1) * HD].astype(F32)
            gradient = turned * cos - turn(turned) * sin
            sums[kind] = sums[kind] + jnp.sum(gradient * hat, axis=0, keepdims=True)
            gained = gradient * gains[kind]
            parts.append(
                (
                    inverse[here, j : j + 1]
                    * (gained - hat * jnp.mean(gained * hat, axis=1, keepdims=True))
                ).astype(BF16)
            )
        for g in range(KV):
            parts.append(value_grad[g, here, :].astype(BF16))
        low = jnp.concatenate(parts, axis=1)
        in_low[dynamic_block(there), :] = low
        if i == 0:
            copies.finish([in_copy])
        partial[i] = nt(low, w_in[...]).astype(BF16)
        copies.start_choice(partial.at[i], keep_hbm, send_hbm, there)
    sums = jnp.concatenate(sums, axis=0)
    high = sums.astype(BF16).astype(F32)
    riders = [high, sums - high, jnp.zeros((PART // X - 4, HD), F32)] * X
    riders = jnp.concatenate(riders, axis=0).astype(BF16)
    copies.finish([first_copy])
    pair_width = in_width - Q_WIDTH
    pair_outs = (pair0, pair1, pair2, pair3)
    for z in range(Z):
        product = tn(first_rows[:, block(z)], in_low[:, Q_WIDTH:]).astype(BF16)
        for y in range(Y):
            k = lax.rem(y + 4 - place_ref[2], 4)
            part = pl.ds(z * PART, PART)
            pair_result[k, part, :pair_width] = product[y * PART : (y + 1) * PART]
            pair_result[k, part, pair_width:] = riders
    for k in (2, 1, 3, 0):
        copies.start(pair_result.at[k], pair_outs[k])
    query_outs = (query0, query1, query2, query3)
    for k in (2, 1, 3, 0):
        z = lax.rem(place_ref[1] + k, 4)
        columns = pl.ds(pl.multiple_of(z * ROWS, ROWS), ROWS)
        query_result[k] = tn(first_rows[:, columns], in_low[:, :Q_WIDTH]).astype(BF16)
        copies.start(query_result.at[k], query_outs[k])
    copies.finish()


def shaped(shape, dtype=BF16):
    return jax.ShapeDtypeStruct(shape, dtype)


def call(kernel, operands, results, scratch, copies, cost, small=None, free=(), weight=1.0):
    in_specs = [pl.BlockSpec(memory_space=pltpu.HBM)] * len(operands)
    chosen = {0: pltpu.SMEM} if small is None else small
    for index, space in chosen.items():
        in_specs[index] = pl.BlockSpec(memory_space=space)
    for index in free:
        in_specs[index] = pl.BlockSpec(memory_space=pl.ANY)
    out_specs = [pl.BlockSpec(memory_space=pltpu.HBM)] * len(results)
    operands = [
        x if index in chosen or index in free else pltpu.with_memory_space_constraint(x, pltpu.HBM)
        for index, x in enumerate(operands)
    ]
    flops, transcendentals = cost
    moved = sum(math.prod(a.shape) * a.dtype.itemsize for a in (*operands, *results))
    return pl.pallas_call(
        kernel,
        out_shape=[pltpu.HBM(r.shape, r.dtype) for r in results],
        in_specs=in_specs,
        out_specs=out_specs,
        scratch_shapes=[pltpu.VMEM(s, d) for s, d in scratch]
        + [pltpu.SemaphoreType.DMA((copies,))],
        compiler_params=pltpu.CompilerParams(vmem_limit_bytes=40 * MIB),
        cost_estimate=pl.CostEstimate(
            flops=int(flops * weight),
            bytes_accessed=int(moved * weight),
            transcendentals=int(transcendentals * weight),
        ),
    )(*operands)


def product(left, weight, start=0):
    (tree, depth), width = left.shape, weight.shape[0]
    pair = shaped((2, ROWS, width))
    return call(
        functools.partial(product_kernel, start=start),
        (left, weight),
        (pair, pair),
        (((tree, depth), BF16), ((width, depth), BF16), ((GROUP, ROWS, width), BF16)),
        1 + 2 * GROUP,
        (2 * tree * depth * width, 0),
        small={},
        weight=0.05,
    )


def outer(*pairs):
    pairs = [(left if isinstance(left, tuple) else (left,), right) for left, right in pairs]
    operands = [a for left, right in pairs for a in (*left, right)]
    tree, width = pairs[0][1].shape[0], sum(right.shape[1] for _, right in pairs)
    depth = pairs[0][0][0].shape[1]
    result = (depth // PART, PART, width)
    scratch = [((tree, a.shape[1]), BF16) for left, right in pairs for a in (left[0], right)]
    pieces = tuple(len(left) for left, _ in pairs)
    return call(
        functools.partial(outer_kernel, pieces=pieces),
        operands,
        (shaped(result),),
        scratch + [(result, BF16)],
        (sum(pieces) + 1) * (depth // ROWS) + len(pieces),
        (2 * tree * depth * width, 0),
        small={},
        free=tuple(range(4)) if pieces == (4,) else (),
        weight=0.05,
    )[0]


def local(
    layer_input,
    cotangent,
    parents,
    offsets,
    w_query,
    w_key,
    w_value,
    w_output,
    w_gate,
    w_up,
    w_down,
    norm_attn,
    norm_mlp,
    query_gain,
    key_gain,
):
    tree = GROUP * ROWS
    width = layer_input.shape[1]
    ff_width = w_gate.shape[1]
    in_width = Q_WIDTH + 2 * K_WIDTH
    fsdp_index = lax.axis_index("fsdp")
    place = jnp.stack([lax.axis_index("tp"), fsdp_index // (Y * X), fsdp_index // X % Y])
    place = place.astype(jnp.int32)

    w_early = jnp.concatenate([w_query, w_key, w_value, w_output.T], axis=1)
    gains = gather_small(jnp.stack([norm_attn, norm_mlp]))
    early_other, gains = lax.optimization_barrier((swapped(w_early), gains))
    early = gather_plane(in_order(w_early, early_other))
    inverse_one = lax.rsqrt(jnp.mean(layer_input * layer_input, axis=1, keepdims=True) + EPSILON)
    normed_one = layer_input * inverse_one
    gain_attn, gain_mlp = gains[0][:, None], gains[1][:, None]
    first_low, out_low, gains = lax.optimization_barrier(
        (normed_one.astype(BF16), cotangent.astype(BF16), gains)
    )
    row_gains = gather_gains(gains)
    first_pieces = gather_rows(first_low)
    low_across = lax.ppermute(out_low, "tp", flip(2))
    row_ancestry, member, path_position = tree_tables(parents[0], offsets[0], tree)
    cosine, sine = rotary(path_position)
    query_extra, key_extra = score_terms(row_ancestry, member)
    head_gains = jnp.pad(jnp.stack([query_gain, key_gain]), ((0, 6), (0, 0)))
    row_gains = jnp.pad(row_gains, ((0, 6), (0, 0)))
    w_late = jnp.concatenate([w_gate, w_up, w_down.T], axis=1)
    w_late, row_gains, first_pieces, cosine, sine, query_extra, key_extra = (
        lax.optimization_barrier(
            (w_late, row_gains, first_pieces, cosine, sine, query_extra, key_extra)
        )
    )
    late = gather_plane(in_order(w_late, swapped(w_late)))
    pair_shape = (2, ROWS, width)
    attention_flops = 2 * tree * tree * HD * HEADS
    (
        queries,
        keys,
        values,
        attended,
        query_hat,
        key_hat,
        inverse,
        first_rows,
        keep,
        send,
    ) = call(
        attention_kernel,
        (
            place,
            *first_pieces,
            early,
            cosine,
            sine,
            query_extra,
            key_extra,
            head_gains,
            row_gains,
        ),
        (
            shaped((HEADS, tree, 2 * HD)),
            shaped((KV, tree, 2 * HD)),
            shaped((KV, tree, 2 * HD)),
            shaped((tree, Q_WIDTH)),
            shaped((tree, Q_WIDTH)),
            shaped((tree, K_WIDTH)),
            shaped((tree, HD), F32),
            shaped((tree, width)),
            shaped(pair_shape),
            shaped(pair_shape),
        ),
        (
            ((tree, width), BF16),
            ((width, in_width), BF16),
            ((width, Q_WIDTH), BF16),
            ((tree, HD), F32),
            ((tree, HD), F32),
            ((tree, HD), BF16),
            ((tree, HD), BF16),
            ((HEADS, tree, 2 * HD), BF16),
            ((KV, tree, 2 * HD), BF16),
            ((KV, tree, 2 * HD), BF16),
            ((tree, Q_WIDTH), BF16),
            ((tree, Q_WIDTH), BF16),
            ((tree, K_WIDTH), BF16),
            ((tree, HD), F32),
            ((GROUP, ROWS, width), BF16),
        ),
        2 + 4 + 4 + 4 + GROUP * (5 + HEADS + 2 * KV),
        (2 * tree * width * (in_width + Q_WIDTH) + 4 * attention_flops, HEADS * tree * tree),
        small={0: pltpu.SMEM, 10: pltpu.VMEM, 11: pltpu.VMEM},
        free=(1, 2, 3, 4),
    )
    keep, send, low_across = lax.optimization_barrier((keep, send, low_across))
    low_pieces = (
        out_low,
        lax.ppermute(out_low, "tp", flip(1)),
        low_across,
        lax.ppermute(low_across, "tp", flip(1)),
    )
    mid_rows = layer_input + scatter_rows(keep, send)
    inverse_two = lax.rsqrt(jnp.mean(mid_rows * mid_rows, axis=1, keepdims=True) + EPSILON)
    normed_two = mid_rows * inverse_two
    second_pieces = gather_rows(normed_two.astype(BF16))
    second_rows, out_low, activated, gate_up_low, grad_keep, grad_send = call(
        mlp_kernel,
        (*second_pieces, *low_pieces, late, row_gains),
        (
            shaped((tree, width)),
            shaped((tree, width)),
            shaped((tree, ff_width)),
            shaped((tree, 2 * ff_width)),
            shaped(pair_shape),
            shaped(pair_shape),
        ),
        (
            ((tree, width), BF16),
            ((tree, width), BF16),
            ((width, 2 * ff_width), BF16),
            ((width, ff_width), BF16),
            ((tree, ff_width), BF16),
            ((tree, 2 * ff_width), BF16),
            ((GROUP, ROWS, width), BF16),
        ),
        2 + 4 * GROUP + 3 * GROUP,
        (10 * tree * width * ff_width, tree * ff_width),
        small={9: pltpu.VMEM},
        free=(0, 1, 2, 3),
    )
    grad_own, grad_other = add_cores(grad_keep, lax.ppermute(grad_send, "tp", flip(1)))
    grad_other = lax.ppermute(grad_other, "tp", flip(2))
    mlp_blocks = outer((second_rows, gate_up_low), (out_low, activated))
    grad_other, mlp_blocks = lax.optimization_barrier((grad_other, mlp_blocks))
    mlp_sums = scatter_plane(mlp_blocks.reshape(width, 3 * ff_width))
    second_grad = grad_own + grad_other.astype(F32)
    mid_grad = cotangent + norm_back(
        second_grad * row_gains[1:2], normed_two, inverse_two
    )
    mid_low = mid_grad.astype(BF16)
    across = lax.ppermute(mid_low, "tp", flip(2))
    beside = lax.ppermute(mid_low, "tp", flip(1))
    out_keep, out_send = product(activated, late, 2 * ff_width)
    across, out_keep, out_send = lax.optimization_barrier((across, out_keep, out_send))
    mid_pieces = (mid_low, beside, across, lax.ppermute(across, "tp", flip(1)))
    out_send = lax.ppermute(out_send, "tp", flip(1))
    out_blocks, mid_pieces = lax.optimization_barrier(
        (outer((tuple(mid_pieces), attended)), tuple(mid_pieces))
    )
    out_blocks = exchange_plane(out_blocks)
    *in_blocks, first_keep, first_send = call(
        backward_kernel,
        (
            place,
            *mid_pieces,
            early,
            attended,
            queries,
            keys,
            values,
            query_hat,
            key_hat,
            inverse,
            cosine,
            sine,
            first_rows,
            head_gains,
        ),
        (
            *(shaped((ROWS, Q_WIDTH)),) * 4,
            *(shaped((ROWS, 2 * K_WIDTH + HD)),) * 4,
            shaped(pair_shape),
            shaped(pair_shape),
        ),
        (
            ((tree, width), BF16),
            ((width, Q_WIDTH), BF16),
            ((tree, Q_WIDTH), BF16),
            ((HEADS, tree, 2 * HD), BF16),
            ((KV, tree, 2 * HD), BF16),
            ((KV, tree, 2 * HD), BF16),
            ((tree, Q_WIDTH), BF16),
            ((tree, K_WIDTH), BF16),
            ((tree, HD), F32),
            ((tree, HD), F32),
            ((tree, HD), F32),
            ((HEADS, tree, 2 * HD), BF16),
            ((KV, tree, HD), F32),
            ((KV, tree, HD), F32),
            ((KV, GROUP, HD, 2 * ROWS), F32),
            ((tree, in_width), BF16),
            ((tree, width), BF16),
            ((4, ROWS, Q_WIDTH), BF16),
            ((4, ROWS, 2 * K_WIDTH + HD), BF16),
            ((width, in_width), BF16),
            ((GROUP, ROWS, width), BF16),
        ),
        1 + 4 + 1 + 3 + 5 + 2 + GROUP + 8,
        (2 * tree * width * (Q_WIDTH + 2 * in_width) + 7 * attention_flops, HEADS * tree * tree),
        small={0: pltpu.SMEM, 16: pltpu.VMEM},
        free=(1, 2, 3, 4),
        weight=3.0,
    )
    in_blocks, out_keep, out_send, out_blocks = lax.optimization_barrier(
        (in_blocks, out_keep, out_send, out_blocks)
    )
    first_grad = scatter_rows(first_keep, first_send)
    layer_output = mid_rows + scatter_chips(*add_cores(out_keep, out_send))
    query_sum = scatter_line(add_line(send_line(in_blocks[:4], "z")), "y")
    pair_sum = scatter_line(add_line(send_line(in_blocks[4:], "y")), "z")
    query_sum, out_blocks = lax.optimization_barrier((query_sum, out_blocks))
    out_sum = jnp.sum(out_blocks.astype(F32), axis=0)
    shard = scatter_pair(
        jnp.concatenate([query_sum, pair_sum, out_sum, mlp_sums.astype(F32)], axis=1)
    )
    widths = (in_width + HD, Q_WIDTH, 2 * ff_width, ff_width)
    ends = [sum(widths[: k + 1]) for k in range(len(widths))]
    in_shard, out_shard, mix_shard, down_shard = jnp.split(shard, ends[:-1], axis=1)
    gain_rows = in_shard[:4, in_width:]
    gain_row = (gain_rows[:2] + gain_rows[2:]).reshape(2 * HD)
    in_shard = in_shard[:, :in_width]
    input_grad = mid_grad + norm_back(first_grad * row_gains[0:1], normed_one, inverse_one)

    def products(weight, shard):
        return jnp.sum(weight.astype(F32) * shard, axis=1)

    query_shard = in_shard[:, :Q_WIDTH]
    key_shard = in_shard[:, Q_WIDTH : Q_WIDTH + K_WIDTH]
    value_shard = in_shard[:, Q_WIDTH + K_WIDTH :]
    gate_shard, up_shard = mix_shard[:, :ff_width], mix_shard[:, ff_width:]
    attn_part = (
        products(w_query, query_shard)
        + products(w_key, key_shard)
        + products(w_value, value_shard)
    )
    mlp_part = products(w_gate, gate_shard) + products(w_up, up_shard)
    sums = sum_group(jnp.concatenate([gain_row, attn_part, mlp_part]))
    own = lax.axis_index("tp") * norm_attn.shape[0]
    norm_attn_grad = lax.dynamic_slice_in_dim(sums, 2 * HD + own, norm_attn.shape[0])
    norm_mlp_grad = lax.dynamic_slice_in_dim(
        sums, 2 * HD + attn_part.shape[0] + own, norm_mlp.shape[0]
    )
    return (
        layer_output,
        input_grad,
        query_shard * gain_attn,
        key_shard * gain_attn,
        value_shard * gain_attn,
        out_shard.T,
        gate_shard * gain_mlp,
        up_shard * gain_mlp,
        down_shard.T,
        norm_attn_grad,
        norm_mlp_grad,
        sums[:HD],
        sums[HD : 2 * HD],
    )


def solution(mesh):
    in_specs = (
        P(("fsdp", "tp"), None),
        P(("fsdp", "tp"), None),
        P("fsdp", None),
        P("fsdp", None),
        P("fsdp", "tp"),
        P("fsdp", "tp"),
        P("fsdp", "tp"),
        P("tp", "fsdp"),
        P("fsdp", "tp"),
        P("fsdp", "tp"),
        P("tp", "fsdp"),
        P(("fsdp", "tp")),
        P(("fsdp", "tp")),
        P(),
        P(),
    )
    out_specs = (
        P(("fsdp", "tp"), None),
        P(("fsdp", "tp"), None),
        P("fsdp", "tp"),
        P("fsdp", "tp"),
        P("fsdp", "tp"),
        P("tp", "fsdp"),
        P("fsdp", "tp"),
        P("fsdp", "tp"),
        P("tp", "fsdp"),
        P(("fsdp", "tp")),
        P(("fsdp", "tp")),
        P(),
        P(),
    )
    return jax.shard_map(local, mesh=mesh, in_specs=in_specs, out_specs=out_specs, check_vma=False)
```
